32 devices in a mesh: grp: 2 (over x), ma: 4 (over y, core), row: 4 (over z).
Axes of the slice: x: 2, y: 2, z: 4, core: 2. Of those that a mesh axis runs over, the one named last changes fastest.
Arguments:
- spectra: bfloat16 [512, 2, 513, 128], P(('grp', 'ma', 'row')), parts along dimension 0, may hold values from -6 to 6
- pair_low: int32 [256], replicated, may hold values from 0 to 255, each once
- legendre: bfloat16 [256, 513, 1024], P(('ma', 'row')), may hold values from -0.25 to 0.25
- dlegendre: bfloat16 [256, 513, 1024], P(('ma', 'row')), may hold values from -0.25 to 0.25
- base_flow: float32 [256, 1024], P(('grp', 'row'), 'ma'), parts along dimension 0, may hold values from -6 to 6
- lat_weights: float32 [1024], P('ma'), may hold values from 0.3 to 3
- to_eigen: bfloat16 [128, 128], replicated, may hold values from -0.5 to 0.5
- from_eigen: bfloat16 [128, 128], replicated, may hold values from -0.5 to 0.5
- decay_rates: float32 [128], replicated, may hold values from 0.1 to 10
Outputs:
- new_spectra: bfloat16 [512, 2, 513, 128], P(('grp', 'ma', 'row')), parts along dimension 0
The draws below stay inside these ranges and needn't reach their ends.
There are 2 independent parts, one for each index of `grp`. The reference program is written for one: setup_inputs(seed, part) draws one part's arguments, and reference() takes and returns one part's arrays. A program takes and returns all parts, laid end to end along the dimension named above; an argument that names none is the same for every part. Nothing has to cross between parts.
Inputs may be any that keep to these rules, and one draw needn't show every extreme that they name: Pair p packs order pair_low[p] and order 512 - 1 - pair_low[p]; every value appears exactly once.
All inputs are finite; a program needn't handle non-finite values.
Results may differ from the reference program's by a relative error of at most 0.009.
Values may be sent and summed in bfloat16 or wider, within the bound.
No kernel may reach another device: no remote copies, remote signals or barrier semaphores. Data moves between devices by JAX's collectives and lax.ppermute only.
A program may use at most 384 MiB of HBM per device.

```python
import math
import jax
import jax.numpy as jnp
from jax import lax

NR = 128
NLAT = 1024
NPAIR = 256
NS = 513


def block_levels(stream_key, shape, cuts, smallest, high):
    factor_of = 1.0
    for axis_at, parts in cuts:
        heights = jax.random.uniform(jax.random.fold_in(jax.random.fold_in(stream_key, 6), axis_at), (parts,), jnp.float32, smallest / len(cuts), high / len(cuts))
        factor_of = factor_of * jnp.repeat(jnp.exp(heights), shape[axis_at] // parts).reshape((-1,) + (1,) * (len(shape) - 1 - axis_at))
    return factor_of


def bell_draw(own_key, dims, width, bound, shards=(), kind=jnp.bfloat16):
    array = jax.random.normal(own_key, dims, jnp.float32) * width
    if len(shards) > 0:
        array = block_levels(own_key, dims, shards, -0.22, 0.18) * array
    return jnp.clip(array, min=-bound, max=bound).astype(kind)


def setup_inputs(seed: int = 0, part: int = 0) -> dict:
    seeds = jax.random.split(jax.random.key(seed), 10)
    part_keys = jax.random.split(jax.random.fold_in(seeds[9], part), 10)
    spectra = bell_draw(part_keys[0], (NPAIR, 2, NS, NR), 1.0, 6.0, ((0, 16),))
    pair_low = jax.random.permutation(seeds[1], NPAIR).astype(jnp.int32)
    legendre = bell_draw(seeds[2], (NPAIR, NS, NLAT), NS ** -0.5, 0.25, ((0, 16),))
    dlegendre = bell_draw(seeds[3], (NPAIR, NS, NLAT), NS ** -0.5, 0.25, ((0, 16),))
    base_flow = bell_draw(part_keys[4], (NR, NLAT), 1.0, 6.0, ((0, 4), (1, 4)), jnp.float32)
    lat_weights = jnp.clip(jnp.exp(math.log(3.0) - 2.3025851 * jax.random.uniform(seeds[5], (NLAT,), jnp.float32) ** block_levels(seeds[5], (NLAT,), ((0, 4),), -0.2, 0.2)), 0.3, 3.0)
    to_eigen = bell_draw(seeds[6], (NR, NR), NR ** -0.5, 0.5)
    from_eigen = bell_draw(seeds[7], (NR, NR), NR ** -0.5, 0.5)
    decay_rates = jnp.clip(jnp.exp(jax.random.uniform(seeds[8], (NR,), jnp.float32, math.log(0.1), math.log(10.0))), 0.1, 10.0)
    return {"spectra": spectra, "pair_low": pair_low, "legendre": legendre, "dlegendre": dlegendre, "base_flow": base_flow, "lat_weights": lat_weights, "to_eigen": to_eigen, "from_eigen": from_eigen, "decay_rates": decay_rates}


time_step = 0.5
horizontal_scale = 4.0

def slot_layout(pair_low, n_slots):
    n_orders = n_slots - 1
    slot_ids = jnp.arange(n_slots, dtype=jnp.int32)
    low_side = slot_ids[None, :] < (n_orders - pair_low)[:, None]
    degree = jnp.where(low_side, pair_low[:, None] + slot_ids[None, :], slot_ids[None, :] - 1).astype(jnp.int32)
    order_masks = jnp.stack([low_side, jnp.logical_not(low_side)], axis=1)
    return (order_masks, degree)

def order_tables(pair_low, n_orders):
    n_lon = 2 * n_orders
    orders = jnp.stack([pair_low, n_orders - 1 - pair_low], axis=1).astype(jnp.int32)
    points = jnp.arange(n_lon, dtype=jnp.int32)
    phase_index = orders[:, :, None] * points[None, None, :] % n_lon
    radians = phase_index.astype(jnp.float32) * (2.0 * math.pi / n_lon)
    cosine_values = jnp.cos(radians)
    sine_values = jnp.sin(radians)
    stacked = jnp.stack([cosine_values, -sine_values], axis=2)
    synth_table = (stacked / math.sqrt(n_orders)).astype(jnp.bfloat16)
    analysis_table = (stacked / math.sqrt(n_lon)).astype(jnp.bfloat16)
    return (synth_table, analysis_table)

def reference(spectra, pair_low, legendre, dlegendre, base_flow, lat_weights, to_eigen, from_eigen, decay_rates):
    n_slots = spectra.shape[2]
    n_orders = n_slots - 1
    order_masks, degree = slot_layout(pair_low, n_slots)
    mask_float = order_masks.astype(jnp.float32)

    def synthesize(inputs):
        coeffs, order_flags, leg_rows, slope_rows = inputs
        masked = order_flags[:, None, :, None] * coeffs.astype(jnp.float32)[None]
        main_part = jnp.einsum('ocsr,st->ocrt', masked, leg_rows.astype(jnp.float32))
        slope_part = jnp.einsum('ocsr,st->ocrt', masked, slope_rows.astype(jnp.float32))
        return (main_part.astype(jnp.bfloat16), slope_part.astype(jnp.bfloat16))
    main_lat, slope_lat = lax.map(synthesize, (spectra, mask_float, legendre, dlegendre))
    synth_table, analysis_table = order_tables(pair_low, n_orders)
    synth_float = synth_table.astype(jnp.float32)
    analysis_float = analysis_table.astype(jnp.float32)

    def physical(inputs):
        main_level, slope_level, base_level = inputs
        main_grid = jnp.einsum('poct,pocn->tn', main_level.astype(jnp.float32), synth_float)
        slope_grid = jnp.einsum('poct,pocn->tn', slope_level.astype(jnp.float32), synth_float)
        product = (main_grid * (slope_grid + base_level[:, None])).astype(jnp.bfloat16)
        product_modes = jnp.einsum('tn,pocn->poct', product.astype(jnp.float32), analysis_float)
        return (product_modes * lat_weights).astype(jnp.bfloat16)
    level_modes = lax.map(physical, (jnp.moveaxis(main_lat, 3, 0), jnp.moveaxis(slope_lat, 3, 0), base_flow))
    product_modes = jnp.moveaxis(level_modes, 0, 3)

    def analyze(inputs):
        pair_modes, order_flags, leg_rows = inputs
        partial_coeffs = jnp.einsum('ocrt,st->ocsr', pair_modes.astype(jnp.float32), leg_rows.astype(jnp.float32))
        return lax.optimization_barrier(jnp.sum(order_flags[:, None, :, None] * partial_coeffs, axis=0))
    nonlinear = lax.map(analyze, (product_modes, mask_float, legendre))
    right_side = (spectra.astype(jnp.float32) + time_step * nonlinear).astype(jnp.bfloat16)
    eigen_coeffs = jnp.einsum('pcsr,kr->pcsk', right_side.astype(jnp.float32), to_eigen.astype(jnp.float32))
    degree_float = degree.astype(jnp.float32)
    factor = 1.0 + horizontal_scale * degree_float * (degree_float + 1.0) / float(n_orders * n_orders)
    factor = factor[:, :, None] + decay_rates[None, None, :]
    scaled = (eigen_coeffs / factor[:, None]).astype(jnp.bfloat16)
    result = jnp.einsum('pcsk,rk->pcsr', scaled.astype(jnp.float32), from_eigen.astype(jnp.float32))
    return result.astype(jnp.bfloat16)
```

```python
import functools
import math

import jax
import jax.numpy as jnp
from jax import lax
from jax.experimental import pallas as pl
from jax.experimental.pallas import tpu as pltpu
from jax.sharding import PartitionSpec as P

time_step = 0.5
horizontal_scale = 4.0
VMEM_BYTES = 56 * 2**20
MAIN_CUTS = (1, 3)
LAST_CUTS = (3, 1)


def params():
    return pltpu.CompilerParams(vmem_limit_bytes=VMEM_BYTES)


def cost(flops, nbytes):
    return pl.CostEstimate(flops=int(flops), bytes_accessed=int(nbytes), transcendentals=0)


def dot(a, b, a_dim=1, b_dim=0):
    return lax.dot_general(
        a, b, (((a_dim,), (b_dim,)), ((), ())), preferred_element_type=jnp.float32
    )


def split_orders(values, edge, half):
    n_orders = values.shape[0] - 1
    ids = lax.broadcasted_iota(jnp.int32, (n_orders, values.shape[1]), 0)
    body = values[0:n_orders]
    low = jnp.where(ids < edge, body, 0.0)
    high = jnp.where(ids[half:] >= edge, body[half:], 0.0)
    high = jnp.where(ids[half:] == half, values[n_orders:], high)
    return low.astype(jnp.bfloat16), high.astype(jnp.bfloat16)


def upper_rows(table_ref, p, half):
    n_orders = table_ref.shape[1] - 1
    upper = table_ref[p, half:n_orders].astype(jnp.float32)
    ids = lax.broadcasted_iota(jnp.int32, upper.shape, 0)
    last = table_ref[p, n_orders:].astype(jnp.float32)
    return jnp.where(ids == 0, last, upper).astype(jnp.bfloat16)


def synth_kernel(first, split, pos_ref, low_ref, s_ref, l_ref, *refs):
    outs, scratch = refs[-1 - split : -1], refs[-1]
    unit, _, n_slots, n_levels = s_ref.shape
    n_lat = l_ref.shape[2]
    n_orders = n_slots - 1
    half = n_orders // 2
    kl = 4 * unit
    for p in range(unit):
        edge = n_orders - low_ref[pos_ref[0] + first + pl.program_id(0) * unit + p]
        sides = [split_orders(s_ref[p, c].astype(jnp.float32), edge, half) for c in range(2)]
        results = (
            dot(l_ref[p, 0:n_orders], jnp.concatenate([sides[0][0], sides[1][0]], axis=1), 0, 0),
            dot(
                upper_rows(l_ref, p, half),
                jnp.concatenate([sides[0][1], sides[1][1]], axis=1),
                0,
                0,
            ),
        )
        for o in range(2):
            for c in range(2):
                start = p * 4 + o * 2 + c
                scratch[pl.ds(start, n_lat, stride=kl), :] = results[o][
                    :, c * n_levels : (c + 1) * n_levels
                ]
    n_dest, step = outs[0].shape[:2]
    for d in range(n_dest):
        for h in range(split):
            start = (d * split + h) * step * kl
            block = scratch[start : start + step * kl].astype(jnp.bfloat16)
            outs[h][d] = block.reshape(step, kl, n_levels)


def synthesize(pos, pair_low, spectra, table, first, count, unit, n_dest, split, after):
    _, _, n_slots, n_levels = spectra.shape
    n_lat = table.shape[2]
    lat_here = n_lat // n_dest
    kl = 4 * unit
    out_shape = (n_dest, lat_here // split, 4 * count, n_levels)
    at = first // unit
    flops = 2 * count * 2 * n_levels * n_slots * 1.5 * n_lat
    nbytes = 2 * (count * 2 * n_slots * n_levels + count * n_slots * n_lat + split * math.prod(out_shape))
    return pl.pallas_call(
        functools.partial(synth_kernel, first, split),
        grid_spec=pltpu.PrefetchScalarGridSpec(
            num_scalar_prefetch=2,
            grid=(count // unit,),
            in_specs=[
                pl.BlockSpec((unit, 2, n_slots, n_levels), lambda p, pos, low: (at + p, 0, 0, 0)),
                pl.BlockSpec((unit, n_slots, n_lat), lambda p, pos, low: (at + p, 0, 0)),
            ]
            + [pl.BlockSpec(memory_space=pl.ANY)] * len(after),
            out_specs=[
                pl.BlockSpec(
                    (n_dest, lat_here // split, kl, n_levels), lambda p, pos, low: (0, 0, p, 0)
                )
            ]
            * split,
            scratch_shapes=[pltpu.VMEM((n_lat * kl, n_levels), jnp.float32)],
        ),
        out_shape=[jax.ShapeDtypeStruct(out_shape, jnp.bfloat16)] * split,
        compiler_params=params(),
        cost_estimate=cost(flops, nbytes),
        name="synthesize",
    )(pos, pair_low, spectra, table, *after)


def gather_columns(refs):
    columns = []
    for t in range(refs[0].shape[1]):
        rows = [ref[:, t].reshape(-1, ref.shape[3]) for ref in refs]
        columns.append(jnp.concatenate(rows, axis=0))
    return jnp.concatenate(columns, axis=1)


def main_grid_kernel(table_ref, *refs):
    refs[-1][...] = dot(table_ref[...], gather_columns(refs[:-1]))


def product_kernel(table_ref, main_ref, base_ref, *refs):
    slope = dot(table_ref[...], gather_columns(refs[:-1]))
    refs[-1][...] = (main_ref[...] * (slope + base_ref[...])).astype(jnp.bfloat16)


def to_grid(table, chunks, main=None, base=None, part=0):
    n_lon, n_coeffs = table.shape
    lat_here, n_levels = chunks[0].shape[1], chunks[0].shape[3]
    step = min(4, lat_here)
    cells = lat_here * n_levels
    wide = pl.BlockSpec((n_lon, step * n_levels), lambda t: (0, t))
    skip = part * (lat_here // step)
    whole = pl.BlockSpec((n_lon, step * n_levels), lambda t: (0, skip + t))
    chunk_specs = [
        pl.BlockSpec((c.shape[0], step, c.shape[2], c.shape[3]), lambda t: (0, t, 0, 0))
        for c in chunks
    ]
    table_spec = pl.BlockSpec((n_lon, n_coeffs), lambda t: (0, 0))
    flops = 2 * n_lon * n_coeffs * cells
    if main is None:
        body, first_specs, first = main_grid_kernel, [table_spec], (table,)
        out_type = jnp.float32
    else:
        base_spec = pl.BlockSpec((1, step * n_levels), lambda t: (0, skip + t))
        body, first_specs, first = product_kernel, [table_spec, whole, base_spec], (table, main, base)
        out_type = jnp.bfloat16
    return pl.pallas_call(
        body,
        grid=(lat_here // step,),
        in_specs=first_specs + chunk_specs,
        out_specs=wide,
        out_shape=jax.ShapeDtypeStruct((n_lon, cells), out_type),
        compiler_params=params(),
        cost_estimate=cost(flops, 2 * n_coeffs * cells + 4 * n_lon * cells),
        name="to_grid",
    )(*first, *chunks)


def modes_kernel(table_ref, product_ref, weight_ref, *refs):
    out_ref, scratch = refs[-2:]
    n_dest, kl, step, n_levels = out_ref.shape
    rows = n_dest * kl
    modes = dot(table_ref[...], product_ref[...]) * weight_ref[...]
    for t in range(step):
        scratch[pl.ds(t, rows, stride=step), :] = modes[:, t * n_levels : (t + 1) * n_levels]
    out_ref[...] = scratch[...].astype(jnp.bfloat16).reshape(out_ref.shape)


def to_modes(table, product, weights, n_dest, n_levels, part, after):
    n_coeffs, n_lon = table.shape
    cells = product.shape[1]
    lat_here = cells // n_levels
    kl = n_coeffs // n_dest
    step = min(16, lat_here)
    skip = part * (lat_here // step)
    return pl.pallas_call(
        modes_kernel,
        grid=(lat_here // step,),
        in_specs=[
            pl.BlockSpec((n_coeffs, n_lon), lambda t: (0, 0)),
            pl.BlockSpec((n_lon, step * n_levels), lambda t: (0, t)),
            pl.BlockSpec((1, step * n_levels), lambda t: (0, skip + t)),
        ]
        + [pl.BlockSpec(memory_space=pl.ANY)] * len(after),
        out_specs=pl.BlockSpec((n_dest, kl, step, n_levels), lambda t: (0, 0, t, 0)),
        out_shape=jax.ShapeDtypeStruct((n_dest, kl, lat_here, n_levels), jnp.bfloat16),
        scratch_shapes=[pltpu.VMEM((n_coeffs * step, n_levels), jnp.float32)],
        compiler_params=params(),
        cost_estimate=cost(2 * n_coeffs * n_lon * cells, 2 * cells * (n_lon + n_coeffs)),
        name="to_modes",
    )(table, product, weights, *after)


def finish_kernel(
    first, split, pos_ref, low_ref, l_ref, s_ref, to_ref, from_ref, decay_ref, *refs
):
    m_refs, (out_ref, scratch) = refs[:split], refs[-2:]
    n_levels = m_refs[0].shape[3]
    n_lat = l_ref.shape[2]
    n_slots = l_ref.shape[1]
    n_orders = n_slots - 1
    half = n_orders // 2
    low = low_ref[pos_ref[0] + first + pl.program_id(0)]
    edge = n_orders - low
    sides = []
    for o in range(2):
        columns = []
        for c in range(2):
            parts = [m_ref[:, o * 2 + c] for m_ref in m_refs]
            columns.append(jnp.concatenate(parts, axis=1).reshape(n_lat, n_levels))
        sides.append(jnp.concatenate(columns, axis=1))
    one = dot(l_ref[0, 0:n_orders], sides[0])
    two = dot(upper_rows(l_ref, 0, half), sides[1])
    scratch[0:half] = one[0:half]
    ids = lax.broadcasted_iota(jnp.int32, two.shape, 0) + half
    scratch[half:n_orders] = jnp.where(ids < edge, one[half:], two)
    scratch[n_orders:n_slots] = two[0:1]
    slots = lax.broadcasted_iota(jnp.int32, (n_slots, 1), 0)
    degree = jnp.where(slots < edge, slots + low, slots - 1).astype(jnp.float32)
    factor = 1.0 + horizontal_scale * degree * (degree + 1.0) / float(n_orders * n_orders)
    factor = factor + decay_ref[...]
    for c in range(2):
        nonlinear = scratch[:, c * n_levels : (c + 1) * n_levels]
        right = s_ref[0, c].astype(jnp.float32) + time_step * nonlinear
        eigen = dot(right.astype(jnp.bfloat16), to_ref[...])
        scaled = (eigen / factor).astype(jnp.bfloat16)
        out_ref[0, c] = dot(scaled, from_ref[...]).astype(jnp.bfloat16)


def finish(pos, pair_low, modes, table, spectra, to_t, from_t, decay, first, count, out):
    n_slots, n_lat = table.shape[1:]
    n_levels = spectra.shape[3]
    mode_specs = [
        pl.BlockSpec(
            (x.shape[0], 4, x.shape[2], n_levels),
            functools.partial(lambda skip, p, pos, low: (0, skip + p, 0, 0), first - begin),
        )
        for begin, x in modes
    ]
    modes = [x for _, x in modes]
    pair_spec = pl.BlockSpec((1, 2, n_slots, n_levels), lambda p, pos, low: (first + p, 0, 0, 0))
    square = pl.BlockSpec((n_levels, n_levels), lambda p, pos, low: (0, 0))
    in_specs = [
        pl.BlockSpec((1, n_slots, n_lat), lambda p, pos, low: (first + p, 0, 0)),
        pair_spec,
        square,
        square,
        pl.BlockSpec((1, n_levels), lambda p, pos, low: (0, 0)),
        *mode_specs,
    ]
    operands = [table, spectra, to_t, from_t, decay, *modes]
    aliases = {}
    if out is not None:
        in_specs.append(pl.BlockSpec(memory_space=pl.ANY))
        operands.append(out)
        aliases = {len(operands) + 1: 0}
    flops = 2 * count * 2 * n_levels * n_slots * (1.5 * n_lat + 2 * n_levels)
    nbytes = 2 * (count * 4 * n_lat * n_levels + count * n_slots * (n_lat + 4 * n_levels))
    return pl.pallas_call(
        functools.partial(finish_kernel, first, len(modes)),
        grid_spec=pltpu.PrefetchScalarGridSpec(
            num_scalar_prefetch=2,
            grid=(count,),
            in_specs=in_specs,
            out_specs=pair_spec,
            scratch_shapes=[pltpu.VMEM((n_slots, 2 * n_levels), jnp.float32)],
        ),
        out_shape=jax.ShapeDtypeStruct(spectra.shape, jnp.bfloat16),
        input_output_aliases=aliases,
        compiler_params=params(),
        cost_estimate=cost(flops, nbytes),
        name="finish",
    )(pos, pair_low, *operands)


def order_tables(low, n_orders):
    n_lon = 2 * n_orders
    orders = jnp.stack([low, n_orders - 1 - low], axis=1)
    points = jnp.arange(n_lon, dtype=jnp.int32)
    phase_index = orders[:, :, None] * points[None, None, :] % n_lon
    radians = phase_index.astype(jnp.float32) * (2.0 * math.pi / n_lon)
    return jnp.stack([jnp.cos(radians), -jnp.sin(radians)], axis=2)


def cut_units(units, unit, sizes):
    if sum(sizes) != units:
        sizes = [units]
    ranges = []
    first = 0
    for size in sizes:
        ranges.append((first, size * unit))
        first += size * unit
    return ranges


def on_device(
    spectra,
    pair_low,
    legendre,
    dlegendre,
    base_flow,
    lat_weights,
    to_eigen,
    from_eigen,
    decay_rates,
):
    pairs_here, _, n_slots, n_levels = spectra.shape
    n_orders = n_slots - 1
    n_lat = legendre.shape[2]
    n_rows = lax.axis_size("row")
    n_dest = lax.axis_size("ma") * n_rows
    lat_here = n_lat // n_dest
    row = lax.axis_index("row")
    here = lax.axis_index("ma") * n_rows + row
    pos = (here * pairs_here).astype(jnp.int32).reshape(1)
    unit = min(4, pairs_here)
    units = pairs_here // unit
    main_cuts = cut_units(units, unit, MAIN_CUTS)
    last_cuts = cut_units(units, unit, LAST_CUTS)
    whole = [(0, pairs_here)]
    split = 2 if lat_here % 32 == 0 else 1

    def exchange(x):
        return lax.all_to_all(x, ("ma", "row"), split_axis=0, concat_axis=0, tiled=True)

    main_lat = []
    after = []
    for first, count in main_cuts:
        (lat,) = synthesize(
            pos, pair_low, spectra, legendre, first, count, unit, n_dest, 1, after
        )
        after = [lat]
        main_lat.append(exchange(lat))
    slopes = synthesize(
        pos, pair_low, spectra, dlegendre, 0, pairs_here, unit, n_dest, split, main_lat[:1]
    )
    slope_lat = [exchange(lat) for lat in slopes]

    table = order_tables(pair_low, n_orders).reshape(n_dest, pairs_here * 4, 2 * n_orders)
    synth_table = (table / math.sqrt(n_orders)).astype(jnp.bfloat16)
    analysis_table = (table / math.sqrt(2 * n_orders)).astype(jnp.bfloat16)

    def rows_of(which, ranges):
        parts = [
            which[:, 4 * f : 4 * (f + c)].reshape(-1, 2 * n_orders) for f, c in ranges
        ]
        return jnp.concatenate(parts, axis=0)

    base = lax.all_to_all(base_flow, "row", split_axis=1, concat_axis=0, tiled=True)
    base = base.T.reshape(1, lat_here * n_levels)
    weights = lax.dynamic_slice_in_dim(lat_weights, row * lat_here, lat_here)
    weights = jnp.repeat(weights, n_levels).reshape(1, lat_here * n_levels)

    main_grid = to_grid(rows_of(synth_table, main_cuts).T, main_lat)
    slope_table = rows_of(synth_table, whole).T
    arrived = []
    for part, lat in enumerate(slope_lat):
        product = to_grid(slope_table, [lat], main_grid, base, part)
        pieces = []
        for first, count in last_cuts if part == split - 1 else whole:
            rows = rows_of(analysis_table, [(first, count)])
            modes = to_modes(rows, product, weights, n_dest, n_levels, part, [])
            pieces.append((first, exchange(modes)))
        arrived.append(pieces)

    to_t, from_t, decay = to_eigen.T, from_eigen.T, decay_rates[None, :]
    out = None
    for n, (first, count) in enumerate(last_cuts):
        modes = [pieces[0] for pieces in arrived[:-1]] + [arrived[-1][n]]
        out = finish(
            pos,
            pair_low,
            modes,
            legendre,
            spectra,
            to_t,
            from_t,
            decay,
            first,
            count,
            out,
        )
    return out


def solution(mesh):
    in_specs = (
        P(("grp", "ma", "row"), None, None, None),
        P(),
        P(("ma", "row"), None, None),
        P(("ma", "row"), None, None),
        P(("grp", "row"), "ma"),
        P("ma"),
        P(),
        P(),
        P(),
    )
    out_specs = P(("grp", "ma", "row"), None, None, None)
    return jax.shard_map(
        on_device, mesh=mesh, in_specs=in_specs, out_specs=out_specs, check_vma=False
    )
```

```python
import functools
import math

import jax
import jax.numpy as jnp
from jax import lax
from jax.experimental import pallas as pl
from jax.experimental.pallas import tpu as pltpu
from jax.sharding import PartitionSpec as P

time_step = 0.5
horizontal_scale = 4.0
VMEM_BYTES = 56 * 2**20
MAIN_CUTS = (1, 3)
LAST_CUTS = (3, 1)


def params():
    return pltpu.CompilerParams(vmem_limit_bytes=VMEM_BYTES)


def cost(flops, nbytes):
    return pl.CostEstimate(flops=int(flops), bytes_accessed=int(nbytes), transcendentals=0)


def dot(a, b, a_dim=1, b_dim=0):
    return lax.dot_general(
        a, b, (((a_dim,), (b_dim,)), ((), ())), preferred_element_type=jnp.float32
    )


def split_orders(values, edge, half):
    n_orders = values.shape[0] - 1
    ids = lax.broadcasted_iota(jnp.int32, (n_orders, values.shape[1]), 0)
    body = values[0:n_orders]
    low = jnp.where(ids < edge, body, 0.0)
    high = jnp.where(ids[half:] >= edge, body[half:], 0.0)
    high = jnp.where(ids[half:] == half, values[n_orders:], high)
    return low.astype(jnp.bfloat16), high.astype(jnp.bfloat16)


def upper_rows(table_ref, p, half):
    n_orders = table_ref.shape[1] - 1
    upper = table_ref[p, half:n_orders].astype(jnp.float32)
    ids = lax.broadcasted_iota(jnp.int32, upper.shape, 0)
    last = table_ref[p, n_orders:].astype(jnp.float32)
    return jnp.where(ids == 0, last, upper).astype(jnp.bfloat16)


def synth_kernel(first, split, pos_ref, low_ref, s_ref, l_ref, *refs):
    outs, scratch = refs[-1 - split : -1], refs[-1]
    unit, _, n_slots, n_levels = s_ref.shape
    n_lat = l_ref.shape[2]
    n_orders = n_slots - 1
    half = n_orders // 2
    kl = 4 * unit
    for p in range(unit):
        edge = n_orders - low_ref[pos_ref[0] + first + pl.program_id(0) * unit + p]
        sides = [split_orders(s_ref[p, c].astype(jnp.float32), edge, half) for c in range(2)]
        results = (
            dot(l_ref[p, 0:n_orders], jnp.concatenate([sides[0][0], sides[1][0]], axis=1), 0, 0),
            dot(
                upper_rows(l_ref, p, half),
                jnp.concatenate([sides[0][1], sides[1][1]], axis=1),
                0,
                0,
            ),
        )
        for o in range(2):
            for c in range(2):
                start = p * 4 + o * 2 + c
                scratch[pl.ds(start, n_lat, stride=kl), :] = results[o][
                    :, c * n_levels : (c + 1) * n_levels
                ]
    n_dest, step = outs[0].shape[:2]
    for d in range(n_dest):
        for h in range(split):
            start = (d * split + h) * step * kl
            block = scratch[start : start + step * kl].astype(jnp.bfloat16)
            outs[h][d] = block.reshape(step, kl, n_levels)


def synthesize(pos, pair_low, spectra, table, first, count, unit, n_dest, split, after):
    _, _, n_slots, n_levels = spectra.shape
    n_lat = table.shape[2]
    lat_here = n_lat // n_dest
    kl = 4 * unit
    out_shape = (n_dest, lat_here // split, 4 * count, n_levels)
    at = first // unit
    flops = 2 * count * 2 * n_levels * n_slots * 1.5 * n_lat
    nbytes = 2 * (count * 2 * n_slots * n_levels + count * n_slots * n_lat + split * math.prod(out_shape))
    return pl.pallas_call(
        functools.partial(synth_kernel, first, split),
        grid_spec=pltpu.PrefetchScalarGridSpec(
            num_scalar_prefetch=2,
            grid=(count // unit,),
            in_specs=[
                pl.BlockSpec((unit, 2, n_slots, n_levels), lambda p, pos, low: (at + p, 0, 0, 0)),
                pl.BlockSpec((unit, n_slots, n_lat), lambda p, pos, low: (at + p, 0, 0)),
            ]
            + [pl.BlockSpec(memory_space=pl.ANY)] * len(after),
            out_specs=[
                pl.BlockSpec(
                    (n_dest, lat_here // split, kl, n_levels), lambda p, pos, low: (0, 0, p, 0)
                )
            ]
            * split,
            scratch_shapes=[pltpu.VMEM((n_lat * kl, n_levels), jnp.float32)],
        ),
        out_shape=[jax.ShapeDtypeStruct(out_shape, jnp.bfloat16)] * split,
        compiler_params=params(),
        cost_estimate=cost(flops, nbytes),
        name="synthesize",
    )(pos, pair_low, spectra, table, *after)


def tile_kernel(
    first, split, unit, pos_ref, low_ref, s_ref, x_ref, *refs
):
    outs = refs[-4 - split : -4]
    low_side, high_side, rows, scratch = refs[-4:]
    _, _, n_slots, n_levels = s_ref.shape
    n_orders = n_slots - 1
    half = n_orders // 2
    pairs, lanes = x_ref.shape[1:]
    kl = 4 * unit
    begin = first + pl.program_id(0) * unit
    inside = lax.rem(begin, pairs)

    @pl.when(pl.program_id(1) == 0)
    def _():
        for p in range(unit):
            edge = n_orders - low_ref[pos_ref[0] + begin + p]
            for c in range(2):
                low, high = split_orders(s_ref[p, c].astype(jnp.float32), edge, half)
                low_side[p, :, c * n_levels : (c + 1) * n_levels] = low
                high_side[p, :, c * n_levels : (c + 1) * n_levels] = high

    rows[...] = x_ref[...].astype(jnp.float32).reshape(n_slots * pairs, lanes)
    ids = lax.broadcasted_iota(jnp.int32, (half, lanes), 0)
    for p in range(unit):
        body = rows[pl.ds(inside + p, n_orders, stride=pairs), :]
        last = rows[pl.ds(n_orders * pairs + inside + p, 1), :]
        upper = jnp.where(ids == 0, last, body[half:]).astype(jnp.bfloat16)
        results = (
            dot(body.astype(jnp.bfloat16), low_side[p], 0, 0),
            dot(upper, high_side[p], 0, 0),
        )
        for o in range(2):
            for c in range(2):
                scratch[pl.ds(p * 4 + o * 2 + c, lanes, stride=kl), :] = results[o][
                    :, c * n_levels : (c + 1) * n_levels
                ]
    n_dest, step = outs[0].shape[:2]
    for d in range(n_dest):
        for h in range(split):
            start = (d * split + h) * step * kl
            block = scratch[start : start + step * kl].astype(jnp.bfloat16)
            outs[h][d] = block.reshape(step, kl, n_levels)


def synthesize_tiles(pos, pair_low, spectra, table, first, count, unit, n_dest, split, after):
    _, _, n_slots, n_levels = spectra.shape
    n_lat = table.shape[2]
    lat_here = n_lat // n_dest
    lanes, pairs = 128, 8
    n_orders = n_slots - 1
    kl = 4 * unit
    out_shape = (n_dest, lat_here // split, 4 * count, n_levels)
    at = first // unit
    flops = 2 * count * 2 * n_levels * n_slots * 1.5 * n_lat
    nbytes = 2 * (count // unit * n_slots * pairs * n_lat + split * math.prod(out_shape))
    return pl.pallas_call(
        functools.partial(tile_kernel, first, split, unit),
        grid_spec=pltpu.PrefetchScalarGridSpec(
            num_scalar_prefetch=2,
            grid=(count // unit, n_lat // lanes),
            in_specs=[
                pl.BlockSpec(
                    (unit, 2, n_slots, n_levels), lambda u, t, pos, low: (at + u, 0, 0, 0)
                ),
                pl.BlockSpec(
                    (n_slots, pairs, lanes),
                    lambda u, t, pos, low: (0, (first + u * unit) // pairs, t),
                ),
            ]
            + [pl.BlockSpec(memory_space=pl.ANY)] * len(after),
            out_specs=[
                pl.BlockSpec(
                    (lanes // lat_here, lat_here // split, kl, n_levels),
                    lambda u, t, pos, low: (t, 0, u, 0),
                )
            ]
            * split,
            scratch_shapes=[
                pltpu.VMEM((unit, n_orders, 2 * n_levels), jnp.bfloat16),
                pltpu.VMEM((unit, n_orders // 2, 2 * n_levels), jnp.bfloat16),
                pltpu.VMEM((n_slots * pairs, lanes), jnp.float32),
                pltpu.VMEM((lanes * kl, n_levels), jnp.float32),
            ],
        ),
        out_shape=[jax.ShapeDtypeStruct(out_shape, jnp.bfloat16)] * split,
        compiler_params=params(),
        cost_estimate=cost(flops, nbytes),
        name="synthesize_tiles",
    )(pos, pair_low, spectra, table, *after)


def gather_columns(refs):
    columns = []
    for t in range(refs[0].shape[1]):
        rows = [ref[:, t].reshape(-1, ref.shape[3]) for ref in refs]
        columns.append(jnp.concatenate(rows, axis=0))
    return jnp.concatenate(columns, axis=1)


def main_grid_kernel(table_ref, *refs):
    refs[-1][...] = dot(table_ref[...], gather_columns(refs[:-1]))


def product_kernel(table_ref, main_ref, base_ref, *refs):
    slope = dot(table_ref[...], gather_columns(refs[:-1]))
    refs[-1][...] = (main_ref[...] * (slope + base_ref[...])).astype(jnp.bfloat16)


def to_grid(table, chunks, main=None, base=None, part=0):
    n_lon, n_coeffs = table.shape
    lat_here, n_levels = chunks[0].shape[1], chunks[0].shape[3]
    step = min(4, lat_here)
    cells = lat_here * n_levels
    wide = pl.BlockSpec((n_lon, step * n_levels), lambda t: (0, t))
    skip = part * (lat_here // step)
    whole = pl.BlockSpec((n_lon, step * n_levels), lambda t: (0, skip + t))
    chunk_specs = [
        pl.BlockSpec((c.shape[0], step, c.shape[2], c.shape[3]), lambda t: (0, t, 0, 0))
        for c in chunks
    ]
    table_spec = pl.BlockSpec((n_lon, n_coeffs), lambda t: (0, 0))
    flops = 2 * n_lon * n_coeffs * cells
    if main is None:
        body, first_specs, first = main_grid_kernel, [table_spec], (table,)
        out_type = jnp.float32
    else:
        base_spec = pl.BlockSpec((1, step * n_levels), lambda t: (0, skip + t))
        body, first_specs, first = product_kernel, [table_spec, whole, base_spec], (table, main, base)
        out_type = jnp.bfloat16
    return pl.pallas_call(
        body,
        grid=(lat_here // step,),
        in_specs=first_specs + chunk_specs,
        out_specs=wide,
        out_shape=jax.ShapeDtypeStruct((n_lon, cells), out_type),
        compiler_params=params(),
        cost_estimate=cost(flops, 2 * n_coeffs * cells + 4 * n_lon * cells),
        name="to_grid",
    )(*first, *chunks)


def modes_kernel(table_ref, product_ref, weight_ref, *refs):
    out_ref, scratch = refs[-2:]
    n_dest, kl, step, n_levels = out_ref.shape
    rows = n_dest * kl
    modes = dot(table_ref[...], product_ref[...]) * weight_ref[...]
    for t in range(step):
        scratch[pl.ds(t, rows, stride=step), :] = modes[:, t * n_levels : (t + 1) * n_levels]
    out_ref[...] = scratch[...].astype(jnp.bfloat16).reshape(out_ref.shape)


def to_modes(table, product, weights, n_dest, n_levels, part, after):
    n_coeffs, n_lon = table.shape
    cells = product.shape[1]
    lat_here = cells // n_levels
    kl = n_coeffs // n_dest
    step = min(16, lat_here)
    skip = part * (lat_here // step)
    return pl.pallas_call(
        modes_kernel,
        grid=(lat_here // step,),
        in_specs=[
            pl.BlockSpec((n_coeffs, n_lon), lambda t: (0, 0)),
            pl.BlockSpec((n_lon, step * n_levels), lambda t: (0, t)),
            pl.BlockSpec((1, step * n_levels), lambda t: (0, skip + t)),
        ]
        + [pl.BlockSpec(memory_space=pl.ANY)] * len(after),
        out_specs=pl.BlockSpec((n_dest, kl, step, n_levels), lambda t: (0, 0, t, 0)),
        out_shape=jax.ShapeDtypeStruct((n_dest, kl, lat_here, n_levels), jnp.bfloat16),
        scratch_shapes=[pltpu.VMEM((n_coeffs * step, n_levels), jnp.float32)],
        compiler_params=params(),
        cost_estimate=cost(2 * n_coeffs * n_lon * cells, 2 * cells * (n_lon + n_coeffs)),
        name="to_modes",
    )(table, product, weights, *after)


def finish_kernel(
    first, split, pos_ref, low_ref, l_ref, s_ref, to_ref, from_ref, decay_ref, *refs
):
    m_refs, (out_ref, scratch) = refs[:split], refs[-2:]
    n_levels = m_refs[0].shape[3]
    n_lat = l_ref.shape[2]
    n_slots = l_ref.shape[1]
    n_orders = n_slots - 1
    half = n_orders // 2
    low = low_ref[pos_ref[0] + first + pl.program_id(0)]
    edge = n_orders - low
    sides = []
    for o in range(2):
        columns = []
        for c in range(2):
            parts = [m_ref[:, o * 2 + c] for m_ref in m_refs]
            columns.append(jnp.concatenate(parts, axis=1).reshape(n_lat, n_levels))
        sides.append(jnp.concatenate(columns, axis=1))
    one = dot(l_ref[0, 0:n_orders], sides[0])
    two = dot(upper_rows(l_ref, 0, half), sides[1])
    scratch[0:half] = one[0:half]
    ids = lax.broadcasted_iota(jnp.int32, two.shape, 0) + half
    scratch[half:n_orders] = jnp.where(ids < edge, one[half:], two)
    scratch[n_orders:n_slots] = two[0:1]
    slots = lax.broadcasted_iota(jnp.int32, (n_slots, 1), 0)
    degree = jnp.where(slots < edge, slots + low, slots - 1).astype(jnp.float32)
    factor = 1.0 + horizontal_scale * degree * (degree + 1.0) / float(n_orders * n_orders)
    factor = factor + decay_ref[...]
    for c in range(2):
        nonlinear = scratch[:, c * n_levels : (c + 1) * n_levels]
        right = s_ref[0, c].astype(jnp.float32) + time_step * nonlinear
        eigen = dot(right.astype(jnp.bfloat16), to_ref[...])
        scaled = (eigen / factor).astype(jnp.bfloat16)
        out_ref[0, c] = dot(scaled, from_ref[...]).astype(jnp.bfloat16)


def finish(pos, pair_low, modes, table, spectra, to_t, from_t, decay, first, count, out):
    n_slots, n_lat = table.shape[1:]
    n_levels = spectra.shape[3]
    mode_specs = [
        pl.BlockSpec(
            (x.shape[0], 4, x.shape[2], n_levels),
            functools.partial(lambda skip, p, pos, low: (0, skip + p, 0, 0), first - begin),
        )
        for begin, x in modes
    ]
    modes = [x for _, x in modes]
    pair_spec = pl.BlockSpec((1, 2, n_slots, n_levels), lambda p, pos, low: (first + p, 0, 0, 0))
    square = pl.BlockSpec((n_levels, n_levels), lambda p, pos, low: (0, 0))
    in_specs = [
        pl.BlockSpec((1, n_slots, n_lat), lambda p, pos, low: (first + p, 0, 0)),
        pair_spec,
        square,
        square,
        pl.BlockSpec((1, n_levels), lambda p, pos, low: (0, 0)),
        *mode_specs,
    ]
    operands = [table, spectra, to_t, from_t, decay, *modes]
    aliases = {}
    if out is not None:
        in_specs.append(pl.BlockSpec(memory_space=pl.ANY))
        operands.append(out)
        aliases = {len(operands) + 1: 0}
    flops = 2 * count * 2 * n_levels * n_slots * (1.5 * n_lat + 2 * n_levels)
    nbytes = 2 * (count * 4 * n_lat * n_levels + count * n_slots * (n_lat + 4 * n_levels))
    return pl.pallas_call(
        functools.partial(finish_kernel, first, len(modes)),
        grid_spec=pltpu.PrefetchScalarGridSpec(
            num_scalar_prefetch=2,
            grid=(count,),
            in_specs=in_specs,
            out_specs=pair_spec,
            scratch_shapes=[pltpu.VMEM((n_slots, 2 * n_levels), jnp.float32)],
        ),
        out_shape=jax.ShapeDtypeStruct(spectra.shape, jnp.bfloat16),
        input_output_aliases=aliases,
        compiler_params=params(),
        cost_estimate=cost(flops, nbytes),
        name="finish",
    )(pos, pair_low, *operands)


def order_tables(low, n_orders):
    n_lon = 2 * n_orders
    orders = jnp.stack([low, n_orders - 1 - low], axis=1)
    points = jnp.arange(n_lon, dtype=jnp.int32)
    phase_index = orders[:, :, None] * points[None, None, :] % n_lon
    radians = phase_index.astype(jnp.float32) * (2.0 * math.pi / n_lon)
    return jnp.stack([jnp.cos(radians), -jnp.sin(radians)], axis=2)


def cut_units(units, unit, sizes):
    if sum(sizes) != units:
        sizes = [units]
    ranges = []
    first = 0
    for size in sizes:
        ranges.append((first, size * unit))
        first += size * unit
    return ranges


def on_device(
    spectra,
    pair_low,
    legendre,
    dlegendre,
    base_flow,
    lat_weights,
    to_eigen,
    from_eigen,
    decay_rates,
):
    pairs_here, _, n_slots, n_levels = spectra.shape
    n_orders = n_slots - 1
    n_lat = legendre.shape[2]
    n_rows = lax.axis_size("row")
    n_dest = lax.axis_size("ma") * n_rows
    lat_here = n_lat // n_dest
    row = lax.axis_index("row")
    here = lax.axis_index("ma") * n_rows + row
    pos = (here * pairs_here).astype(jnp.int32).reshape(1)
    unit = min(4, pairs_here)
    units = pairs_here // unit
    main_cuts = cut_units(units, unit, MAIN_CUTS)
    last_cuts = cut_units(units, unit, LAST_CUTS)
    whole = [(0, pairs_here)]
    split = 2 if lat_here % 32 == 0 else 1

    def exchange(x):
        return lax.all_to_all(x, ("ma", "row"), split_axis=0, concat_axis=0, tiled=True)

    tiles = pairs_here % 8 == 0 and 128 % lat_here == 0

    def lat_functions(rows, first, count, parts, after):
        if tiles:
            body, rows = synthesize_tiles, jnp.transpose(rows, (1, 0, 2))
        else:
            body = synthesize
        own = spectra
        if first == 0 and count == unit:
            own = lax.slice_in_dim(spectra, 0, unit)
        return body(pos, pair_low, own, rows, first, count, unit, n_dest, parts, after)

    main_lat = []
    after = []
    for first, count in main_cuts:
        (lat,) = lat_functions(legendre, first, count, 1, after)
        after = [lat]
        main_lat.append(exchange(lat))
    base = lax.all_to_all(base_flow, "row", split_axis=1, concat_axis=0, tiled=True)
    base = base.T.reshape(1, lat_here * n_levels)

    slopes = lat_functions(dlegendre, 0, pairs_here, split, after)
    slope_lat = [exchange(lat) for lat in slopes]

    table = order_tables(pair_low, n_orders).reshape(n_dest, pairs_here * 4, 2 * n_orders)
    synth_table = (table / math.sqrt(n_orders)).astype(jnp.bfloat16)
    analysis_table = (table / math.sqrt(2 * n_orders)).astype(jnp.bfloat16)

    def rows_of(which, ranges):
        parts = [
            which[:, 4 * f : 4 * (f + c)].reshape(-1, 2 * n_orders) for f, c in ranges
        ]
        return jnp.concatenate(parts, axis=0)

    weights = lax.dynamic_slice_in_dim(lat_weights, row * lat_here, lat_here)
    weights = jnp.repeat(weights, n_levels).reshape(1, lat_here * n_levels)

    main_grid = to_grid(rows_of(synth_table, main_cuts).T, main_lat)
    slope_table = rows_of(synth_table, whole).T
    arrived = []
    for part, lat in enumerate(slope_lat):
        product = to_grid(slope_table, [lat], main_grid, base, part)
        pieces = []
        for first, count in last_cuts if part == split - 1 else whole:
            rows = rows_of(analysis_table, [(first, count)])
            modes = to_modes(rows, product, weights, n_dest, n_levels, part, [])
            pieces.append((first, exchange(modes)))
        arrived.append(pieces)

    to_t, from_t, decay = to_eigen.T, from_eigen.T, decay_rates[None, :]
    out = None
    for n, (first, count) in enumerate(last_cuts):
        modes = [pieces[0] for pieces in arrived[:-1]] + [arrived[-1][n]]
        out = finish(
            pos,
            pair_low,
            modes,
            legendre,
            spectra,
            to_t,
            from_t,
            decay,
            first,
            count,
            out,
        )
    return out


def solution(mesh):
    in_specs = (
        P(("grp", "ma", "row"), None, None, None),
        P(),
        P(("ma", "row"), None, None),
        P(("ma", "row"), None, None),
        P(("grp", "row"), "ma"),
        P("ma"),
        P(),
        P(),
        P(),
    )
    out_specs = P(("grp", "ma", "row"), None, None, None)
    return jax.shard_map(
        on_device, mesh=mesh, in_specs=in_specs, out_specs=out_specs, check_vma=False
    )
```

```python
import functools
import math

import jax
import jax.numpy as jnp
from jax import lax
from jax.experimental import pallas as pl
from jax.experimental.pallas import tpu as pltpu
from jax.sharding import PartitionSpec as P

time_step = 0.5
horizontal_scale = 4.0
VMEM_BYTES = 56 * 2**20
MAIN_CUTS = (1, 3)


def params():
    return pltpu.CompilerParams(vmem_limit_bytes=VMEM_BYTES)


def padded(count):
    return (count // 8 + 2) * 8


def cost(flops, nbytes):
    return pl.CostEstimate(flops=int(flops), bytes_accessed=int(nbytes), transcendentals=0)


def dot(a, b, a_dim=1, b_dim=0):
    return lax.dot_general(
        a, b, (((a_dim,), (b_dim,)), ((), ())), preferred_element_type=jnp.float32
    )


def split_orders(values, edge, half):
    n_orders = values.shape[0] - 1
    ids = lax.broadcasted_iota(jnp.int32, (n_orders, values.shape[1]), 0)
    body = values[0:n_orders]
    low = jnp.where(ids < edge, body, 0.0)
    high = jnp.where(ids[half:] >= edge, body[half:], 0.0)
    high = jnp.where(ids[half:] == half, values[n_orders:], high)
    return low.astype(jnp.bfloat16), high.astype(jnp.bfloat16)


def upper_rows(table_ref, p, half):
    n_orders = table_ref.shape[1] - 1
    upper = table_ref[p, half:n_orders].astype(jnp.float32)
    ids = lax.broadcasted_iota(jnp.int32, upper.shape, 0)
    last = table_ref[p, n_orders:].astype(jnp.float32)
    return jnp.where(ids == 0, last, upper).astype(jnp.bfloat16)


def synth_kernel(first, split, pos_ref, low_ref, s_ref, l_ref, *refs):
    outs, scratch = refs[-1 - split : -1], refs[-1]
    unit, _, n_slots, n_levels = s_ref.shape
    n_lat = l_ref.shape[2]
    n_orders = n_slots - 1
    half = n_orders // 2
    kl = 4 * unit
    for p in range(unit):
        edge = n_orders - low_ref[pos_ref[0] + first + pl.program_id(0) * unit + p]
        sides = [split_orders(s_ref[p, c].astype(jnp.float32), edge, half) for c in range(2)]
        results = (
            dot(l_ref[p, 0:n_orders], jnp.concatenate([sides[0][0], sides[1][0]], axis=1), 0, 0),
            dot(
                upper_rows(l_ref, p, half),
                jnp.concatenate([sides[0][1], sides[1][1]], axis=1),
                0,
                0,
            ),
        )
        for o in range(2):
            for c in range(2):
                start = p * 4 + o * 2 + c
                scratch[pl.ds(start, n_lat, stride=kl), :] = results[o][
                    :, c * n_levels : (c + 1) * n_levels
                ]
    n_dest, step = outs[0].shape[:2]
    for d in range(n_dest):
        for h in range(split):
            start = (d * split + h) * step * kl
            block = scratch[start : start + step * kl].astype(jnp.bfloat16)
            outs[h][d] = block.reshape(step, kl, n_levels)


def synthesize(pos, pair_low, spectra, table, first, count, unit, n_dest, split, after):
    _, _, n_slots, n_levels = spectra.shape
    n_lat = table.shape[2]
    lat_here = n_lat // n_dest
    kl = 4 * unit
    out_shape = (n_dest, lat_here // split, 4 * count, n_levels)
    at = first // unit
    flops = 2 * count * 2 * n_levels * n_slots * 1.5 * n_lat
    nbytes = 2 * (count * 2 * n_slots * n_levels + count * n_slots * n_lat + split * math.prod(out_shape))
    return pl.pallas_call(
        functools.partial(synth_kernel, first, split),
        grid_spec=pltpu.PrefetchScalarGridSpec(
            num_scalar_prefetch=2,
            grid=(count // unit,),
            in_specs=[
                pl.BlockSpec((unit, 2, n_slots, n_levels), lambda p, pos, low: (at + p, 0, 0, 0)),
                pl.BlockSpec((unit, n_slots, n_lat), lambda p, pos, low: (at + p, 0, 0)),
            ]
            + [pl.BlockSpec(memory_space=pl.ANY)] * len(after),
            out_specs=[
                pl.BlockSpec(
                    (n_dest, lat_here // split, kl, n_levels), lambda p, pos, low: (0, 0, p, 0)
                )
            ]
            * split,
            scratch_shapes=[pltpu.VMEM((n_lat * kl, n_levels), jnp.float32)],
        ),
        out_shape=[jax.ShapeDtypeStruct(out_shape, jnp.bfloat16)] * split,
        compiler_params=params(),
        cost_estimate=cost(flops, nbytes),
        name="synthesize",
    )(pos, pair_low, spectra, table, *after)


def tile_kernel(
    first, split, unit, pos_ref, low_ref, s_ref, x_ref, *refs
):
    outs = refs[-5 - split : -5]
    low_side, high_side, rows, scratch, turned = refs[-5:]
    _, n_slots, _, n_levels = s_ref.shape
    n_orders = n_slots - 1
    half = n_orders // 2
    pairs, lanes = x_ref.shape[1:]
    kl = 4 * unit
    begin = first + pl.program_id(0) * unit
    inside = lax.rem(begin, pairs)

    @pl.when(pl.program_id(1) == 0)
    def _():
        for p in range(unit):
            edge = n_orders - low_ref[pos_ref[0] + begin + p]
            turned[0 : 2 * n_slots] = s_ref[p].astype(jnp.float32).reshape(2 * n_slots, n_levels)
            for c in range(2):
                coeffs = turned[pl.ds(c, n_slots, stride=2), :]
                low, high = split_orders(coeffs, edge, half)
                low_side[p, :, c * n_levels : (c + 1) * n_levels] = low
                high_side[p, :, c * n_levels : (c + 1) * n_levels] = high

    rows[0 : n_slots * pairs] = x_ref[...].astype(jnp.float32).reshape(n_slots * pairs, lanes)
    ids = lax.broadcasted_iota(jnp.int32, (half, lanes), 0)
    for p in range(unit):
        body = rows[pl.ds(inside + p, n_orders, stride=pairs), :]
        last = rows[pl.ds(n_orders * pairs + inside + p, 1), :]
        upper = jnp.where(ids == 0, last, body[half:]).astype(jnp.bfloat16)
        results = (
            dot(body.astype(jnp.bfloat16), low_side[p], 0, 0),
            dot(upper, high_side[p], 0, 0),
        )
        for o in range(2):
            for c in range(2):
                scratch[pl.ds(p * 4 + o * 2 + c, lanes, stride=kl), :] = results[o][
                    :, c * n_levels : (c + 1) * n_levels
                ]
    n_dest, step = outs[0].shape[:2]
    for d in range(n_dest):
        for h in range(split):
            start = (d * split + h) * step * kl
            block = scratch[start : start + step * kl].astype(jnp.bfloat16)
            outs[h][d] = block.reshape(step, kl, n_levels)


def synthesize_tiles(pos, pair_low, spectra, table, first, count, unit, n_dest, split, after):
    _, n_slots, _, n_levels = spectra.shape
    n_lat = table.shape[2]
    lat_here = n_lat // n_dest
    lanes, pairs = 128, 8
    n_orders = n_slots - 1
    kl = 4 * unit
    out_shape = (n_dest, lat_here // split, 4 * count, n_levels)
    at = first // unit
    flops = 2 * count * 2 * n_levels * n_slots * 1.5 * n_lat
    nbytes = 2 * (count // unit * n_slots * pairs * n_lat + split * math.prod(out_shape))
    return pl.pallas_call(
        functools.partial(tile_kernel, first, split, unit),
        grid_spec=pltpu.PrefetchScalarGridSpec(
            num_scalar_prefetch=2,
            grid=(count // unit, n_lat // lanes),
            in_specs=[
                pl.BlockSpec(
                    (unit, n_slots, 2, n_levels), lambda u, t, pos, low: (at + u, 0, 0, 0)
                ),
                pl.BlockSpec(
                    (n_slots, pairs, lanes),
                    lambda u, t, pos, low: (0, (first + u * unit) // pairs, t),
                ),
            ]
            + [pl.BlockSpec(memory_space=pl.ANY)] * len(after),
            out_specs=[
                pl.BlockSpec(
                    (lanes // lat_here, lat_here // split, kl, n_levels),
                    lambda u, t, pos, low: (t, 0, u, 0),
                )
            ]
            * split,
            scratch_shapes=[
                pltpu.VMEM((unit, n_orders, 2 * n_levels), jnp.bfloat16),
                pltpu.VMEM((unit, n_orders // 2, 2 * n_levels), jnp.bfloat16),
                pltpu.VMEM((padded(n_slots) * pairs, lanes), jnp.float32),
                pltpu.VMEM((lanes * kl, n_levels), jnp.float32),
                pltpu.VMEM((2 * padded(n_slots), n_levels), jnp.float32),
            ],
        ),
        out_shape=[jax.ShapeDtypeStruct(out_shape, jnp.bfloat16)] * split,
        compiler_params=params(),
        cost_estimate=cost(flops, nbytes),
        name="synthesize_tiles",
    )(pos, pair_low, spectra, table, *after)


def gather_columns(refs):
    columns = []
    for t in range(refs[0].shape[1]):
        rows = [ref[:, t].reshape(-1, ref.shape[3]) for ref in refs]
        columns.append(jnp.concatenate(rows, axis=0))
    return jnp.concatenate(columns, axis=1)


def main_grid_kernel(table_ref, *refs):
    refs[-1][...] = dot(table_ref[...], gather_columns(refs[:-1]))


def product_kernel(table_ref, main_ref, base_ref, *refs):
    slope = dot(table_ref[...], gather_columns(refs[:-1]))
    refs[-1][...] = (main_ref[...] * (slope + base_ref[...])).astype(jnp.bfloat16)


def to_grid(table, chunks, main=None, base=None, part=0):
    n_lon, n_coeffs = table.shape
    lat_here, n_levels = chunks[0].shape[1], chunks[0].shape[3]
    step = min(4, lat_here)
    cells = lat_here * n_levels
    wide = pl.BlockSpec((n_lon, step * n_levels), lambda t: (0, t))
    skip = part * (lat_here // step)
    whole = pl.BlockSpec((n_lon, step * n_levels), lambda t: (0, skip + t))
    chunk_specs = [
        pl.BlockSpec((c.shape[0], step, c.shape[2], c.shape[3]), lambda t: (0, t, 0, 0))
        for c in chunks
    ]
    table_spec = pl.BlockSpec((n_lon, n_coeffs), lambda t: (0, 0))
    flops = 2 * n_lon * n_coeffs * cells
    if main is None:
        body, first_specs, first = main_grid_kernel, [table_spec], (table,)
        out_type = jnp.float32
    else:
        base_spec = pl.BlockSpec((1, step * n_levels), lambda t: (0, skip + t))
        body, first_specs, first = product_kernel, [table_spec, whole, base_spec], (table, main, base)
        out_type = jnp.bfloat16
    return pl.pallas_call(
        body,
        grid=(lat_here // step,),
        in_specs=first_specs + chunk_specs,
        out_specs=wide,
        out_shape=jax.ShapeDtypeStruct((n_lon, cells), out_type),
        compiler_params=params(),
        cost_estimate=cost(flops, 2 * n_coeffs * cells + 4 * n_lon * cells),
        name="to_grid",
    )(*first, *chunks)


def modes_kernel(table_ref, product_ref, weight_ref, *refs):
    out_ref, scratch = refs[-2:]
    n_dest, kl, step, n_levels = out_ref.shape
    rows = n_dest * kl
    modes = dot(table_ref[...], product_ref[...]) * weight_ref[...]
    for t in range(step):
        scratch[pl.ds(t, rows, stride=step), :] = modes[:, t * n_levels : (t + 1) * n_levels]
    out_ref[...] = scratch[...].astype(jnp.bfloat16).reshape(out_ref.shape)


def to_modes(table, product, weights, n_dest, n_levels, part, after):
    n_coeffs, n_lon = table.shape
    cells = product.shape[1]
    lat_here = cells // n_levels
    kl = n_coeffs // n_dest
    step = min(16, lat_here)
    skip = part * (lat_here // step)
    return pl.pallas_call(
        modes_kernel,
        grid=(lat_here // step,),
        in_specs=[
            pl.BlockSpec((n_coeffs, n_lon), lambda t: (0, 0)),
            pl.BlockSpec((n_lon, step * n_levels), lambda t: (0, t)),
            pl.BlockSpec((1, step * n_levels), lambda t: (0, skip + t)),
        ]
        + [pl.BlockSpec(memory_space=pl.ANY)] * len(after),
        out_specs=pl.BlockSpec((n_dest, kl, step, n_levels), lambda t: (0, 0, t, 0)),
        out_shape=jax.ShapeDtypeStruct((n_dest, kl, lat_here, n_levels), jnp.bfloat16),
        scratch_shapes=[pltpu.VMEM((n_coeffs * step, n_levels), jnp.float32)],
        compiler_params=params(),
        cost_estimate=cost(2 * n_coeffs * n_lon * cells, 2 * cells * (n_lon + n_coeffs)),
        name="to_modes",
    )(table, product, weights, *after)


def finish_kernel(
    first, split, pos_ref, low_ref, l_ref, s_ref, to_ref, from_ref, decay_ref, *refs
):
    m_refs, (out_ref, scratch, turned) = refs[:split], refs[-3:]
    n_levels = m_refs[0].shape[3]
    n_lat = l_ref.shape[2]
    n_slots = l_ref.shape[1]
    n_orders = n_slots - 1
    half = n_orders // 2
    low = low_ref[pos_ref[0] + first + pl.program_id(0)]
    edge = n_orders - low
    sides = []
    for o in range(2):
        columns = []
        for c in range(2):
            parts = [m_ref[:, o * 2 + c] for m_ref in m_refs]
            columns.append(jnp.concatenate(parts, axis=1).reshape(n_lat, n_levels))
        sides.append(jnp.concatenate(columns, axis=1))
    one = dot(l_ref[0, 0:n_orders], sides[0])
    two = dot(upper_rows(l_ref, 0, half), sides[1])
    scratch[0:half] = one[0:half]
    ids = lax.broadcasted_iota(jnp.int32, two.shape, 0) + half
    scratch[half:n_orders] = jnp.where(ids < edge, one[half:], two)
    scratch[n_orders:n_slots] = two[0:1]
    slots = lax.broadcasted_iota(jnp.int32, (n_slots, 1), 0)
    degree = jnp.where(slots < edge, slots + low, slots - 1).astype(jnp.float32)
    factor = 1.0 + horizontal_scale * degree * (degree + 1.0) / float(n_orders * n_orders)
    factor = factor + decay_ref[...]
    turned[0 : 2 * n_slots] = s_ref[0].astype(jnp.float32).reshape(2 * n_slots, n_levels)
    spectra = [turned[pl.ds(c, n_slots, stride=2), :] for c in range(2)]
    for c in range(2):
        nonlinear = scratch[:, c * n_levels : (c + 1) * n_levels]
        right = spectra[c] + time_step * nonlinear
        eigen = dot(right.astype(jnp.bfloat16), to_ref[...])
        scaled = (eigen / factor).astype(jnp.bfloat16)
        turned[pl.ds(c, n_slots, stride=2), :] = dot(scaled, from_ref[...])
    out_ref[0] = turned[0 : 2 * n_slots].reshape(n_slots, 2, n_levels).astype(jnp.bfloat16)


def finish(pos, pair_low, modes, table, spectra, to_t, from_t, decay, first, count, out):
    n_slots, n_lat = table.shape[1:]
    n_levels = spectra.shape[3]
    mode_specs = [
        pl.BlockSpec(
            (x.shape[0], 4, x.shape[2], n_levels),
            functools.partial(lambda skip, p, pos, low: (0, skip + p, 0, 0), first - begin),
        )
        for begin, x in modes
    ]
    modes = [x for _, x in modes]
    pair_spec = pl.BlockSpec((1, n_slots, 2, n_levels), lambda p, pos, low: (first + p, 0, 0, 0))
    square = pl.BlockSpec((n_levels, n_levels), lambda p, pos, low: (0, 0))
    in_specs = [
        pl.BlockSpec((1, n_slots, n_lat), lambda p, pos, low: (first + p, 0, 0)),
        pair_spec,
        square,
        square,
        pl.BlockSpec((1, n_levels), lambda p, pos, low: (0, 0)),
        *mode_specs,
    ]
    operands = [table, spectra, to_t, from_t, decay, *modes]
    aliases = {}
    if out is not None:
        in_specs.append(pl.BlockSpec(memory_space=pl.ANY))
        operands.append(out)
        aliases = {len(operands) + 1: 0}
    flops = 2 * count * 2 * n_levels * n_slots * (1.5 * n_lat + 2 * n_levels)
    nbytes = 2 * (count * 4 * n_lat * n_levels + count * n_slots * (n_lat + 4 * n_levels))
    return pl.pallas_call(
        functools.partial(finish_kernel, first, len(modes)),
        grid_spec=pltpu.PrefetchScalarGridSpec(
            num_scalar_prefetch=2,
            grid=(count,),
            in_specs=in_specs,
            out_specs=pair_spec,
            scratch_shapes=[
                pltpu.VMEM((n_slots, 2 * n_levels), jnp.float32),
                pltpu.VMEM((2 * padded(n_slots), n_levels), jnp.float32),
            ],
        ),
        out_shape=jax.ShapeDtypeStruct(spectra.shape, jnp.bfloat16),
        input_output_aliases=aliases,
        compiler_params=params(),
        cost_estimate=cost(flops, nbytes),
        name="finish",
    )(pos, pair_low, *operands)


def order_tables(low, n_orders):
    n_lon = 2 * n_orders
    orders = jnp.stack([low, n_orders - 1 - low], axis=1)
    points = jnp.arange(n_lon, dtype=jnp.int32)
    phase_index = orders[:, :, None] * points[None, None, :] % n_lon
    radians = phase_index.astype(jnp.float32) * (2.0 * math.pi / n_lon)
    return jnp.stack([jnp.cos(radians), -jnp.sin(radians)], axis=2)


def cut_units(units, unit, sizes):
    if sum(sizes) != units:
        sizes = [units]
    ranges = []
    first = 0
    for size in sizes:
        ranges.append((first, size * unit))
        first += size * unit
    return ranges


def on_device(
    spectra,
    pair_low,
    legendre,
    dlegendre,
    base_flow,
    lat_weights,
    to_eigen,
    from_eigen,
    decay_rates,
):
    pairs_here, _, n_slots, n_levels = spectra.shape
    n_orders = n_slots - 1
    n_lat = legendre.shape[2]
    n_rows = lax.axis_size("row")
    n_dest = lax.axis_size("ma") * n_rows
    lat_here = n_lat // n_dest
    row = lax.axis_index("row")
    here = lax.axis_index("ma") * n_rows + row
    pos = (here * pairs_here).astype(jnp.int32).reshape(1)
    unit = min(4, pairs_here)
    units = pairs_here // unit
    main_cuts = cut_units(units, unit, MAIN_CUTS)
    whole = [(0, pairs_here)]
    last_cuts = [(0, pairs_here - 2), (pairs_here - 2, 2)] if pairs_here > 4 else whole
    split = 2 if lat_here % 32 == 0 else 1

    def exchange(x):
        return lax.all_to_all(x, ("ma", "row"), split_axis=0, concat_axis=0, tiled=True)

    tiles = pairs_here % 8 == 0 and 128 % lat_here == 0

    slots_ahead = jnp.transpose(spectra, (0, 2, 1, 3))

    def lat_functions(rows, first, count, parts, after):
        if tiles:
            body, own, rows = synthesize_tiles, slots_ahead, jnp.transpose(rows, (1, 0, 2))
        else:
            body, own = synthesize, spectra
        return body(pos, pair_low, own, rows, first, count, unit, n_dest, parts, after)

    main_lat = []
    after = []
    for first, count in main_cuts:
        (lat,) = lat_functions(legendre, first, count, 1, after)
        after = [lat]
        main_lat.append(exchange(lat))
    base = lax.all_to_all(base_flow, "row", split_axis=1, concat_axis=0, tiled=True)
    base = base.T.reshape(1, lat_here * n_levels)

    slopes = lat_functions(dlegendre, 0, pairs_here, split, after)
    slope_lat = [exchange(lat) for lat in slopes]

    table = order_tables(pair_low, n_orders).reshape(n_dest, pairs_here * 4, 2 * n_orders)
    synth_table = (table / math.sqrt(n_orders)).astype(jnp.bfloat16)
    analysis_table = (table / math.sqrt(2 * n_orders)).astype(jnp.bfloat16)

    def rows_of(which, ranges):
        parts = [
            which[:, 4 * f : 4 * (f + c)].reshape(-1, 2 * n_orders) for f, c in ranges
        ]
        return jnp.concatenate(parts, axis=0)

    weights = lax.dynamic_slice_in_dim(lat_weights, row * lat_here, lat_here)
    weights = jnp.repeat(weights, n_levels).reshape(1, lat_here * n_levels)

    main_grid = to_grid(rows_of(synth_table, main_cuts).T, main_lat)
    slope_table = rows_of(synth_table, whole).T
    arrived = []
    for part, lat in enumerate(slope_lat):
        product = to_grid(slope_table, [lat], main_grid, base, part)
        pieces = []
        for first, count in last_cuts if part == split - 1 else whole:
            rows = rows_of(analysis_table, [(first, count)])
            modes = to_modes(rows, product, weights, n_dest, n_levels, part, [legendre])
            pieces.append((first, exchange(modes)))
        arrived.append(pieces)

    to_t, from_t, decay = to_eigen.T, from_eigen.T, decay_rates[None, :]
    out = None
    for n, (first, count) in enumerate(last_cuts):
        modes = [pieces[0] for pieces in arrived[:-1]] + [arrived[-1][n]]
        out = finish(
            pos,
            pair_low,
            modes,
            legendre,
            slots_ahead,
            to_t,
            from_t,
            decay,
            first,
            count,
            out,
        )
    return jnp.transpose(out, (0, 2, 1, 3))


def solution(mesh):
    in_specs = (
        P(("grp", "ma", "row"), None, None, None),
        P(),
        P(("ma", "row"), None, None),
        P(("ma", "row"), None, None),
        P(("grp", "row"), "ma"),
        P("ma"),
        P(),
        P(),
        P(),
    )
    out_specs = P(("grp", "ma", "row"), None, None, None)
    return jax.shard_map(
        on_device, mesh=mesh, in_specs=in_specs, out_specs=out_specs, check_vma=False
    )
```

```python
import functools
import math

import jax
import jax.numpy as jnp
from jax import lax
from jax.experimental import pallas as pl
from jax.experimental.pallas import tpu as pltpu
from jax.sharding import PartitionSpec as P

time_step = 0.5
horizontal_scale = 4.0
VMEM_BYTES = 56 * 2**20
MAIN_CUTS = (1, 3)


def params():
    return pltpu.CompilerParams(vmem_limit_bytes=VMEM_BYTES)


def padded(count):
    return (count // 8 + 2) * 8


def cost(flops, nbytes):
    return pl.CostEstimate(flops=int(flops), bytes_accessed=int(nbytes), transcendentals=0)


def dot(a, b, a_dim=1, b_dim=0):
    return lax.dot_general(
        a, b, (((a_dim,), (b_dim,)), ((), ())), preferred_element_type=jnp.float32
    )


def split_orders(values, edge, half):
    n_orders = values.shape[0] - 1
    ids = lax.broadcasted_iota(jnp.int32, (n_orders, values.shape[1]), 0)
    body = values[0:n_orders]
    low = jnp.where(ids < edge, body, 0.0)
    high = jnp.where(ids[half:] >= edge, body[half:], 0.0)
    high = jnp.where(ids[half:] == half, values[n_orders:], high)
    return low.astype(jnp.bfloat16), high.astype(jnp.bfloat16)


def upper_rows(table_ref, p, half):
    n_orders = table_ref.shape[1] - 1
    upper = table_ref[p, half:n_orders].astype(jnp.float32)
    ids = lax.broadcasted_iota(jnp.int32, upper.shape, 0)
    last = table_ref[p, n_orders:].astype(jnp.float32)
    return jnp.where(ids == 0, last, upper).astype(jnp.bfloat16)


def synth_kernel(first, split, pos_ref, low_ref, s_ref, l_ref, *refs):
    outs, scratch = refs[-1 - split : -1], refs[-1]
    unit, _, n_slots, n_levels = s_ref.shape
    n_lat = l_ref.shape[2]
    n_orders = n_slots - 1
    half = n_orders // 2
    kl = 4 * unit
    for p in range(unit):
        edge = n_orders - low_ref[pos_ref[0] + first + pl.program_id(0) * unit + p]
        sides = [split_orders(s_ref[p, c].astype(jnp.float32), edge, half) for c in range(2)]
        results = (
            dot(l_ref[p, 0:n_orders], jnp.concatenate([sides[0][0], sides[1][0]], axis=1), 0, 0),
            dot(
                upper_rows(l_ref, p, half),
                jnp.concatenate([sides[0][1], sides[1][1]], axis=1),
                0,
                0,
            ),
        )
        for o in range(2):
            for c in range(2):
                start = p * 4 + o * 2 + c
                scratch[pl.ds(start, n_lat, stride=kl), :] = results[o][
                    :, c * n_levels : (c + 1) * n_levels
                ]
    n_dest, step = outs[0].shape[:2]
    for d in range(n_dest):
        for h in range(split):
            start = (d * split + h) * step * kl
            block = scratch[start : start + step * kl].astype(jnp.bfloat16)
            outs[h][d] = block.reshape(step, kl, n_levels)


def synthesize(pos, pair_low, spectra, table, first, count, unit, n_dest, split, after):
    _, _, n_slots, n_levels = spectra.shape
    n_lat = table.shape[2]
    lat_here = n_lat // n_dest
    kl = 4 * unit
    out_shape = (n_dest, lat_here // split, 4 * count, n_levels)
    at = first // unit
    flops = 2 * count * 2 * n_levels * n_slots * 1.5 * n_lat
    nbytes = 2 * (count * 2 * n_slots * n_levels + count * n_slots * n_lat + split * math.prod(out_shape))
    return pl.pallas_call(
        functools.partial(synth_kernel, first, split),
        grid_spec=pltpu.PrefetchScalarGridSpec(
            num_scalar_prefetch=2,
            grid=(count // unit,),
            in_specs=[
                pl.BlockSpec((unit, 2, n_slots, n_levels), lambda p, pos, low: (at + p, 0, 0, 0)),
                pl.BlockSpec((unit, n_slots, n_lat), lambda p, pos, low: (at + p, 0, 0)),
            ]
            + [pl.BlockSpec(memory_space=pl.ANY)] * len(after),
            out_specs=[
                pl.BlockSpec(
                    (n_dest, lat_here // split, kl, n_levels), lambda p, pos, low: (0, 0, p, 0)
                )
            ]
            * split,
            scratch_shapes=[pltpu.VMEM((n_lat * kl, n_levels), jnp.float32)],
        ),
        out_shape=[jax.ShapeDtypeStruct(out_shape, jnp.bfloat16)] * split,
        compiler_params=params(),
        cost_estimate=cost(flops, nbytes),
        name="synthesize",
    )(pos, pair_low, spectra, table, *after)


def tile_kernel(
    first, split, unit, pos_ref, low_ref, s_ref, x_ref, *refs
):
    outs = refs[-5 - split : -5]
    low_side, high_side, rows, scratch, turned = refs[-5:]
    _, n_slots, _, n_levels = s_ref.shape
    n_orders = n_slots - 1
    half = n_orders // 2
    pairs, lanes = x_ref.shape[1:]
    kl = 4 * unit
    begin = first + pl.program_id(0) * unit
    inside = lax.rem(begin, pairs)

    @pl.when(pl.program_id(1) == 0)
    def _():
        for p in range(unit):
            edge = n_orders - low_ref[pos_ref[0] + begin + p]
            turned[0 : 2 * n_slots] = s_ref[p].astype(jnp.float32).reshape(2 * n_slots, n_levels)
            for c in range(2):
                coeffs = turned[pl.ds(c, n_slots, stride=2), :]
                low, high = split_orders(coeffs, edge, half)
                low_side[p, :, c * n_levels : (c + 1) * n_levels] = low
                high_side[p, :, c * n_levels : (c + 1) * n_levels] = high

    n_tiles, _, tile_lanes = rows.shape
    for tile in range(n_tiles):
        part = x_ref[:, :, tile * tile_lanes : (tile + 1) * tile_lanes].astype(jnp.float32)
        rows[tile, 0 : n_slots * pairs] = part.reshape(n_slots * pairs, tile_lanes)
    ids = lax.broadcasted_iota(jnp.int32, (half, lanes), 0)
    for p in range(unit):
        bodies = [
            rows[tile, pl.ds(inside + p, n_orders, stride=pairs), :] for tile in range(n_tiles)
        ]
        lasts = [
            rows[tile, pl.ds(n_orders * pairs + inside + p, 1), :] for tile in range(n_tiles)
        ]
        body = jnp.concatenate(bodies, axis=1)
        last = jnp.concatenate(lasts, axis=1)
        upper = jnp.where(ids == 0, last, body[half:]).astype(jnp.bfloat16)
        results = (
            dot(body.astype(jnp.bfloat16), low_side[p], 0, 0),
            dot(upper, high_side[p], 0, 0),
        )
        for o in range(2):
            for c in range(2):
                scratch[pl.ds(p * 4 + o * 2 + c, lanes, stride=kl), :] = results[o][
                    :, c * n_levels : (c + 1) * n_levels
                ]
    n_dest, step = outs[0].shape[:2]
    for d in range(n_dest):
        for h in range(split):
            start = (d * split + h) * step * kl
            block = scratch[start : start + step * kl].astype(jnp.bfloat16)
            outs[h][d] = block.reshape(step, kl, n_levels)


def synthesize_tiles(pos, pair_low, spectra, table, first, count, unit, n_dest, split, after):
    _, n_slots, _, n_levels = spectra.shape
    n_lat = table.shape[2]
    lat_here = n_lat // n_dest
    lanes, pairs = 256, 8
    n_orders = n_slots - 1
    kl = 4 * unit
    out_shape = (n_dest, lat_here // split, 4 * count, n_levels)
    at = first // unit
    flops = 2 * count * 2 * n_levels * n_slots * 1.5 * n_lat
    nbytes = 2 * (count // unit * n_slots * pairs * n_lat + split * math.prod(out_shape))
    return pl.pallas_call(
        functools.partial(tile_kernel, first, split, unit),
        grid_spec=pltpu.PrefetchScalarGridSpec(
            num_scalar_prefetch=2,
            grid=(count // unit, n_lat // lanes),
            in_specs=[
                pl.BlockSpec(
                    (unit, n_slots, 2, n_levels), lambda u, t, pos, low: (at + u, 0, 0, 0)
                ),
                pl.BlockSpec(
                    (n_slots, pairs, lanes),
                    lambda u, t, pos, low: (0, (first + u * unit) // pairs, t),
                ),
            ]
            + [pl.BlockSpec(memory_space=pl.ANY)] * len(after),
            out_specs=[
                pl.BlockSpec(
                    (lanes // lat_here, lat_here // split, kl, n_levels),
                    lambda u, t, pos, low: (t, 0, u, 0),
                )
            ]
            * split,
            scratch_shapes=[
                pltpu.VMEM((unit, n_orders, 2 * n_levels), jnp.bfloat16),
                pltpu.VMEM((unit, n_orders // 2, 2 * n_levels), jnp.bfloat16),
                pltpu.VMEM((lanes // 128, padded(n_slots) * pairs, 128), jnp.float32),
                pltpu.VMEM((lanes * kl, n_levels), jnp.float32),
                pltpu.VMEM((2 * padded(n_slots), n_levels), jnp.float32),
            ],
        ),
        out_shape=[jax.ShapeDtypeStruct(out_shape, jnp.bfloat16)] * split,
        compiler_params=params(),
        cost_estimate=cost(flops, nbytes),
        name="synthesize_tiles",
    )(pos, pair_low, spectra, table, *after)


def gather_columns(refs):
    columns = []
    for t in range(refs[0].shape[1]):
        rows = [ref[:, t].reshape(-1, ref.shape[3]) for ref in refs]
        columns.append(jnp.concatenate(rows, axis=0))
    return jnp.concatenate(columns, axis=1)


def main_grid_kernel(table_ref, *refs):
    refs[-1][...] = dot(table_ref[...], gather_columns(refs[:-1]))


def product_kernel(table_ref, main_ref, base_ref, *refs):
    slope = dot(table_ref[...], gather_columns(refs[:-1]))
    refs[-1][...] = (main_ref[...] * (slope + base_ref[...])).astype(jnp.bfloat16)


def to_grid(table, chunks, main=None, base=None, part=0):
    n_lon, n_coeffs = table.shape
    lat_here, n_levels = chunks[0].shape[1], chunks[0].shape[3]
    step = min(4, lat_here)
    cells = lat_here * n_levels
    wide = pl.BlockSpec((n_lon, step * n_levels), lambda t: (0, t))
    skip = part * (lat_here // step)
    whole = pl.BlockSpec((n_lon, step * n_levels), lambda t: (0, skip + t))
    chunk_specs = [
        pl.BlockSpec((c.shape[0], step, c.shape[2], c.shape[3]), lambda t: (0, t, 0, 0))
        for c in chunks
    ]
    table_spec = pl.BlockSpec((n_lon, n_coeffs), lambda t: (0, 0))
    flops = 2 * n_lon * n_coeffs * cells
    if main is None:
        body, first_specs, first = main_grid_kernel, [table_spec], (table,)
        out_type = jnp.float32
    else:
        base_spec = pl.BlockSpec((1, step * n_levels), lambda t: (0, skip + t))
        body, first_specs, first = product_kernel, [table_spec, whole, base_spec], (table, main, base)
        out_type = jnp.bfloat16
    return pl.pallas_call(
        body,
        grid=(lat_here // step,),
        in_specs=first_specs + chunk_specs,
        out_specs=wide,
        out_shape=jax.ShapeDtypeStruct((n_lon, cells), out_type),
        compiler_params=params(),
        cost_estimate=cost(flops, 2 * n_coeffs * cells + 4 * n_lon * cells),
        name="to_grid",
    )(*first, *chunks)


def modes_kernel(table_ref, product_ref, weight_ref, *refs):
    out_ref, scratch = refs[-2:]
    n_dest, kl, step, n_levels = out_ref.shape
    rows = n_dest * kl
    modes = dot(table_ref[...], product_ref[...]) * weight_ref[...]
    for t in range(step):
        scratch[pl.ds(t, rows, stride=step), :] = modes[:, t * n_levels : (t + 1) * n_levels]
    out_ref[...] = scratch[...].astype(jnp.bfloat16).reshape(out_ref.shape)


def to_modes(table, product, weights, n_dest, n_levels, part, after):
    n_coeffs, n_lon = table.shape
    cells = product.shape[1]
    lat_here = cells // n_levels
    kl = n_coeffs // n_dest
    step = min(16, lat_here)
    skip = part * (lat_here // step)
    return pl.pallas_call(
        modes_kernel,
        grid=(lat_here // step,),
        in_specs=[
            pl.BlockSpec((n_coeffs, n_lon), lambda t: (0, 0)),
            pl.BlockSpec((n_lon, step * n_levels), lambda t: (0, t)),
            pl.BlockSpec((1, step * n_levels), lambda t: (0, skip + t)),
        ]
        + [pl.BlockSpec(memory_space=pl.ANY)] * len(after),
        out_specs=pl.BlockSpec((n_dest, kl, step, n_levels), lambda t: (0, 0, t, 0)),
        out_shape=jax.ShapeDtypeStruct((n_dest, kl, lat_here, n_levels), jnp.bfloat16),
        scratch_shapes=[pltpu.VMEM((n_coeffs * step, n_levels), jnp.float32)],
        compiler_params=params(),
        cost_estimate=cost(2 * n_coeffs * n_lon * cells, 2 * cells * (n_lon + n_coeffs)),
        name="to_modes",
    )(table, product, weights, *after)


def finish_kernel(
    first, split, pos_ref, low_ref, l_ref, s_ref, to_ref, from_ref, decay_ref, *refs
):
    m_refs, (out_ref, scratch, turned) = refs[:split], refs[-3:]
    n_levels = m_refs[0].shape[3]
    n_lat = l_ref.shape[2]
    n_slots = l_ref.shape[1]
    n_orders = n_slots - 1
    half = n_orders // 2
    low = low_ref[pos_ref[0] + first + pl.program_id(0)]
    edge = n_orders - low
    sides = []
    for o in range(2):
        columns = []
        for c in range(2):
            parts = [m_ref[:, o * 2 + c] for m_ref in m_refs]
            columns.append(jnp.concatenate(parts, axis=1).reshape(n_lat, n_levels))
        sides.append(jnp.concatenate(columns, axis=1))
    one = dot(l_ref[0, 0:n_orders], sides[0])
    two = dot(upper_rows(l_ref, 0, half), sides[1])
    scratch[0:half] = one[0:half]
    ids = lax.broadcasted_iota(jnp.int32, two.shape, 0) + half
    scratch[half:n_orders] = jnp.where(ids < edge, one[half:], two)
    scratch[n_orders:n_slots] = two[0:1]
    slots = lax.broadcasted_iota(jnp.int32, (n_slots, 1), 0)
    degree = jnp.where(slots < edge, slots + low, slots - 1).astype(jnp.float32)
    factor = 1.0 + horizontal_scale * degree * (degree + 1.0) / float(n_orders * n_orders)
    factor = factor + decay_ref[...]
    turned[0 : 2 * n_slots] = s_ref[0].astype(jnp.float32).reshape(2 * n_slots, n_levels)
    spectra = [turned[pl.ds(c, n_slots, stride=2), :] for c in range(2)]
    for c in range(2):
        nonlinear = scratch[:, c * n_levels : (c + 1) * n_levels]
        right = spectra[c] + time_step * nonlinear
        eigen = dot(right.astype(jnp.bfloat16), to_ref[...])
        scaled = (eigen / factor).astype(jnp.bfloat16)
        turned[pl.ds(c, n_slots, stride=2), :] = dot(scaled, from_ref[...])
    out_ref[0] = turned[0 : 2 * n_slots].reshape(n_slots, 2, n_levels).astype(jnp.bfloat16)


def finish(pos, pair_low, modes, table, spectra, to_t, from_t, decay, first, count, out):
    n_slots, n_lat = table.shape[1:]
    n_levels = spectra.shape[3]
    mode_specs = [
        pl.BlockSpec(
            (x.shape[0], 4, x.shape[2], n_levels),
            functools.partial(lambda skip, p, pos, low: (0, skip + p, 0, 0), first - begin),
        )
        for begin, x in modes
    ]
    modes = [x for _, x in modes]
    pair_spec = pl.BlockSpec((1, n_slots, 2, n_levels), lambda p, pos, low: (first + p, 0, 0, 0))
    square = pl.BlockSpec((n_levels, n_levels), lambda p, pos, low: (0, 0))
    in_specs = [
        pl.BlockSpec((1, n_slots, n_lat), lambda p, pos, low: (first + p, 0, 0)),
        pair_spec,
        square,
        square,
        pl.BlockSpec((1, n_levels), lambda p, pos, low: (0, 0)),
        *mode_specs,
    ]
    operands = [table, spectra, to_t, from_t, decay, *modes]
    aliases = {}
    if out is not None:
        in_specs.append(pl.BlockSpec(memory_space=pl.ANY))
        operands.append(out)
        aliases = {len(operands) + 1: 0}
    flops = 2 * count * 2 * n_levels * n_slots * (1.5 * n_lat + 2 * n_levels)
    nbytes = 2 * (count * 4 * n_lat * n_levels + count * n_slots * (n_lat + 4 * n_levels))
    return pl.pallas_call(
        functools.partial(finish_kernel, first, len(modes)),
        grid_spec=pltpu.PrefetchScalarGridSpec(
            num_scalar_prefetch=2,
            grid=(count,),
            in_specs=in_specs,
            out_specs=pair_spec,
            scratch_shapes=[
                pltpu.VMEM((n_slots, 2 * n_levels), jnp.float32),
                pltpu.VMEM((2 * padded(n_slots), n_levels), jnp.float32),
            ],
        ),
        out_shape=jax.ShapeDtypeStruct(spectra.shape, jnp.bfloat16),
        input_output_aliases=aliases,
        compiler_params=params(),
        cost_estimate=cost(flops, nbytes),
        name="finish",
    )(pos, pair_low, *operands)


def order_tables(low, n_orders):
    n_lon = 2 * n_orders
    orders = jnp.stack([low, n_orders - 1 - low], axis=1)
    points = jnp.arange(n_lon, dtype=jnp.int32)
    phase_index = orders[:, :, None] * points[None, None, :] % n_lon
    radians = phase_index.astype(jnp.float32) * (2.0 * math.pi / n_lon)
    return jnp.stack([jnp.cos(radians), -jnp.sin(radians)], axis=2)


def cut_units(units, unit, sizes):
    if sum(sizes) != units:
        sizes = [units]
    ranges = []
    first = 0
    for size in sizes:
        ranges.append((first, size * unit))
        first += size * unit
    return ranges


def on_device(
    spectra,
    pair_low,
    legendre,
    dlegendre,
    base_flow,
    lat_weights,
    to_eigen,
    from_eigen,
    decay_rates,
):
    pairs_here, _, n_slots, n_levels = spectra.shape
    n_orders = n_slots - 1
    n_lat = legendre.shape[2]
    n_rows = lax.axis_size("row")
    n_dest = lax.axis_size("ma") * n_rows
    lat_here = n_lat // n_dest
    row = lax.axis_index("row")
    here = lax.axis_index("ma") * n_rows + row
    pos = (here * pairs_here).astype(jnp.int32).reshape(1)
    unit = min(4, pairs_here)
    units = pairs_here // unit
    main_cuts = cut_units(units, unit, MAIN_CUTS)
    whole = [(0, pairs_here)]
    last_cuts = [(0, pairs_here - 2), (pairs_here - 2, 2)] if pairs_here > 4 else whole
    split = 2 if lat_here % 32 == 0 else 1

    def exchange(x):
        return lax.all_to_all(x, ("ma", "row"), split_axis=0, concat_axis=0, tiled=True)

    tiles = pairs_here % 8 == 0 and 128 % lat_here == 0 and n_lat % 256 == 0

    slots_ahead = jnp.transpose(spectra, (0, 2, 1, 3))

    def lat_functions(rows, first, count, parts, after):
        if tiles:
            body, own, rows = synthesize_tiles, slots_ahead, jnp.transpose(rows, (1, 0, 2))
        else:
            body, own = synthesize, spectra
        return body(pos, pair_low, own, rows, first, count, unit, n_dest, parts, after)

    main_lat = []
    after = []
    for first, count in main_cuts:
        (lat,) = lat_functions(legendre, first, count, 1, after)
        after = [lat]
        main_lat.append(exchange(lat))
    base = lax.all_to_all(base_flow, "row", split_axis=1, concat_axis=0, tiled=True)
    base = base.T.reshape(1, lat_here * n_levels)

    slopes = lat_functions(dlegendre, 0, pairs_here, split, after)
    slope_lat = [exchange(lat) for lat in slopes]

    table = order_tables(pair_low, n_orders).reshape(n_dest, pairs_here * 4, 2 * n_orders)
    synth_table = (table / math.sqrt(n_orders)).astype(jnp.bfloat16)
    analysis_table = (table / math.sqrt(2 * n_orders)).astype(jnp.bfloat16)

    def rows_of(which, ranges):
        parts = [
            which[:, 4 * f : 4 * (f + c)].reshape(-1, 2 * n_orders) for f, c in ranges
        ]
        return jnp.concatenate(parts, axis=0)

    weights = lax.dynamic_slice_in_dim(lat_weights, row * lat_here, lat_here)
    weights = jnp.repeat(weights, n_levels).reshape(1, lat_here * n_levels)

    main_grid = to_grid(rows_of(synth_table, main_cuts).T, main_lat)
    slope_table = rows_of(synth_table, whole).T
    arrived = []
    for part, lat in enumerate(slope_lat):
        product = to_grid(slope_table, [lat], main_grid, base, part)
        pieces = []
        for first, count in last_cuts if part == split - 1 else whole:
            rows = rows_of(analysis_table, [(first, count)])
            modes = to_modes(rows, product, weights, n_dest, n_levels, part, [legendre])
            pieces.append((first, exchange(modes)))
        arrived.append(pieces)

    to_t, from_t, decay = to_eigen.T, from_eigen.T, decay_rates[None, :]
    out = None
    for n, (first, count) in enumerate(last_cuts):
        modes = [pieces[0] for pieces in arrived[:-1]] + [arrived[-1][n]]
        out = finish(
            pos,
            pair_low,
            modes,
            legendre,
            slots_ahead,
            to_t,
            from_t,
            decay,
            first,
            count,
            out,
        )
    return jnp.transpose(out, (0, 2, 1, 3))


def solution(mesh):
    in_specs = (
        P(("grp", "ma", "row"), None, None, None),
        P(),
        P(("ma", "row"), None, None),
        P(("ma", "row"), None, None),
        P(("grp", "row"), "ma"),
        P("ma"),
        P(),
        P(),
        P(),
    )
    out_specs = P(("grp", "ma", "row"), None, None, None)
    return jax.shard_map(
        on_device, mesh=mesh, in_specs=in_specs, out_specs=out_specs, check_vma=False
    )
```
